1024 devices in a mesh: dp: 32 (over y, z_hi, core), tensor: 32 (over z_lo, x).
Axes of the slice: x: 4, y: 4, z: 32 (z_hi: 4, z_lo: 8; z = z_hi * 8 + z_lo), core: 2. Of those that a mesh axis runs over, the one named last changes fastest.
Arguments:
- out_grad: bfloat16 [12288, 5120], P(('dp', 'tensor')), may hold values from -24 to 24
- gate_pre: bfloat16 [12288, 14336], P('dp', 'tensor'), may hold values from -6 to 6
- up_pre: bfloat16 [12288, 14336], P('dp', 'tensor'), may hold values from -6 to 6
- down_weight: bfloat16 [14336, 5120], P('tensor'), may hold values from -0.078125 to 0.078125
Outputs:
- gate_grad: bfloat16 [12288, 14336], P('dp', 'tensor')
- up_grad: bfloat16 [12288, 14336], P('dp', 'tensor')
- weight_grad: float32 [14336, 5120], P('tensor', 'dp')
The draws below stay inside these ranges and needn't reach their ends.
All inputs are finite; a program needn't handle non-finite values.
Results may differ from the reference program's by a relative error of at most 0.018.
Values may be sent and summed in bfloat16 or wider, within the bound.
A program may use at most 64 MiB of HBM per device.

```python
import jax
import jax.numpy as jnp
from jax import lax

D = 5120
FF = 14336
TOK_REP = 384
TOTAL = 12288
N_DP = 32


def spiked(array, own_key, source, target, parts, factor):
    def block_of(dim):
        return (jnp.arange(array.shape[dim]) // (array.shape[dim] // parts)).reshape((-1,) + (1,) * (array.ndim - 1 - dim))

    one_side = jax.random.permutation(own_key, parts)[block_of(target)]
    other_side = (block_of(target) + parts // 2) % parts
    return jnp.where((block_of(source) == one_side) | (block_of(source) == other_side), factor * array, array)


def steps_of(stream_key, extent, cuts, least, high):
    def one(axis_at, blocks):
        draws = jax.random.uniform(jax.random.fold_in(jax.random.fold_in(stream_key, 6), axis_at), (blocks,), jnp.float32, least / len(cuts), high / len(cuts))
        return jnp.repeat(jnp.exp(draws), extent[axis_at] // blocks).reshape((-1,) + (1,) * (len(extent) - axis_at - 1))

    factor_of = one(*cuts[0])
    for cut in cuts[1:]:
        factor_of = factor_of * one(*cut)
    return factor_of


def normal_values(own_key, dims, width, reach, cuts=(), kind=jnp.bfloat16):
    values = width * jax.random.normal(own_key, dims, jnp.float32)
    if cuts:
        values = values * steps_of(own_key, dims, cuts, -0.22, 0.18)
    return jnp.clip(values, -reach, reach).astype(kind)


def heavy_noise(key, shape, scale, bound, cuts, heavy, kind=jnp.bfloat16):
    values = scale * jax.random.normal(key, shape, jnp.float32)
    if cuts:
        values = values * steps_of(key, shape, cuts, -0.22, 0.18)
    return jnp.clip(spiked(values, jax.random.fold_in(key, 3), *heavy), -bound, bound).astype(kind)


def setup_inputs(seed: int = 0) -> dict:
    arg_keys = jax.random.split(jax.random.key(seed), 5)
    return {
        "out_grad": heavy_noise(arg_keys[0], (TOTAL, D), 1.0, 24.0, ((0, 1024),), (0, 1, 1024, 6.0)),
        "gate_pre": normal_values(arg_keys[1], (TOTAL, FF), 1.0, 6.0, ((0, 32), (1, 32))),
        "up_pre": normal_values(arg_keys[2], (TOTAL, FF), 1.0, 6.0, ((0, 32), (1, 32))),
        "down_weight": normal_values(arg_keys[3], (FF, D), D ** -0.5, 0.078125, ((0, 32),)),
    }


def reference(out_grad, gate_pre, up_pre, down_weight):
    grads_all = out_grad.reshape(N_DP, TOK_REP, D)
    gates_all = gate_pre.reshape(N_DP, TOK_REP, FF)
    ups_all = up_pre.reshape(N_DP, TOK_REP, FF)

    def replica_step(running, pieces):
        grads_out, gate_rows, up_rows = pieces
        gate_wide = gate_rows.astype(jnp.float32)
        up_wide = up_rows.astype(jnp.float32)
        logistic = jax.nn.sigmoid(gate_wide)
        swish = gate_wide * logistic
        hidden = (swish * up_wide).astype(jnp.bfloat16)
        back_grad = jnp.dot(grads_out, down_weight.T, preferred_element_type=jnp.float32)
        up_result = (back_grad * swish).astype(jnp.bfloat16)
        gate_result = (back_grad * up_wide * logistic * (1.0 + gate_wide * (1.0 - logistic))).astype(jnp.bfloat16)
        partial_value = jnp.dot(hidden.T, grads_out, preferred_element_type=jnp.float32).astype(jnp.bfloat16)
        partial_value = lax.optimization_barrier(partial_value).astype(jnp.float32)
        return running + partial_value, (gate_result, up_result)

    start_sum = jnp.zeros((FF, D), jnp.float32)
    summed, outputs = lax.scan(replica_step, start_sum, (grads_all, gates_all, ups_all))
    gate_grad = outputs[0].reshape(TOTAL, FF)
    up_grad = outputs[1].reshape(TOTAL, FF)
    weight_grad = summed * jnp.float32(float(TOTAL) ** -0.5)
    return gate_grad, up_grad, weight_grad
```

```python
import functools

import jax
import jax.numpy as jnp
from jax import lax
from jax.experimental import pallas as pl
from jax.experimental.pallas import tpu as pltpu
from jax.sharding import PartitionSpec as P

MESH = pl.DeviceIdType.MESH
BF = jnp.bfloat16
F32 = jnp.float32

NX = 4
NZ = 8
NK = 5
TOK = 384
OWN = 12
LINE = 48
FFL = 448
HALF = 224
QUARTER = 1280
WIDE = 160
R0 = 64
RR = 112


def tile_columns(load, k):
    sides = []
    for c in range(2):
        if k < 4:
            at = k * 2 * WIDE + c * WIDE
            sides.append(load(at, 128))
        else:
            sides.append(
                jnp.concatenate([load(z * 2 * WIDE + c * WIDE + 128, 32) for z in range(4)], axis=1)
            )
    return sides


def kernel(
    og, gate_hbm, up_hbm, w_hbm,
    gg, ug, wg,
    gate, up, w, wp, ht, xs, asend, arecv, bg, pm, csend, crecv,
    y1s, y1r, y2s, y2r, z1s, z1r, z2s, z2r, zf, pr, q1s, q1r, q2s, q2r,
    lsem, a_s, a_r, l_s, l_r, x_s, x_r, c_s, c_r, y_s, y_r, z_s, z_r,
):
    dp = lax.axis_index("dp")
    tn = lax.axis_index("tensor")
    y, zh, core = dp // 8, (dp // 2) % 4, dp % 2
    zl, x = tn // 4, tn % 4

    def at_x(d):
        return (dp, zl * 4 + (x + d) % 4)

    def at_y(d):
        return (((y + d) % 4) * 8 + zh * 2 + core, tn)

    def at_z(d):
        return (y * 8 + ((zh + d) % 4) * 2 + core, tn)

    def at_line(d):
        return (dp, tn + 4 * d)

    other = (dp + 1 - 2 * core, tn)

    loads = [
        pltpu.make_async_copy(gate_hbm, gate, lsem.at[0]),
        pltpu.make_async_copy(up_hbm, up, lsem.at[1]),
        pltpu.make_async_copy(w_hbm, w, lsem.at[2]),
    ]
    for copy in loads:
        copy.start()

    barrier = pltpu.get_barrier_semaphore()

    def greet(device):
        pl.semaphore_signal(barrier, inc=1, device_id=device, device_id_type=MESH)

    for device in (at_x(1), at_x(2), at_x(3), other, at_y(1), at_y(3), at_z(1), at_z(3)):
        greet(device)

    @pl.when(zl > 0)
    def _():
        greet(at_line(-1))

    @pl.when(zl < NZ - 1)
    def _():
        greet(at_line(1))

    asend[...] = jnp.zeros_like(asend)
    for q in range(4):
        for k in range(NK):
            lo, hi = tile_columns(lambda at, n: og[:, q * QUARTER + at : q * QUARTER + at + n], k)
            asend[q, k, 0:OWN, 0:128] = lo
            asend[q, k, 0:OWN, 128:256] = hi
    inner = jnp.where(zl > 0, 1, 0) + jnp.where(zl < NZ - 1, 1, 0)
    pl.semaphore_wait(barrier, 8 + inner)

    drains = []

    def remote(src, dst, ss, rs, device):
        return pltpu.make_async_remote_copy(
            src_ref=src, dst_ref=dst, send_sem=ss, recv_sem=rs, device_id=device, device_id_type=MESH
        )

    def send(src, dst, ss, rs, device):
        copy = remote(src, dst, ss, rs, device)
        copy.start()
        drains.append(copy)

    def arrived(dst, rs):
        remote(dst, dst, rs, rs, other).wait_recv()

    for d in (2, 1, 3):
        send(asend.at[(x + d) % 4], arecv.at[x], a_s.at[d], a_r.at[d], at_x(d))
    arecv[pl.ds(x, 1)] = asend[pl.ds(x, 1)]

    loads[0].wait()
    loads[1].wait()
    g = gate[...].astype(F32)
    hidden = (g * jax.nn.sigmoid(g) * up[...].astype(F32)).astype(BF)
    ht[...] = hidden.T
    for d in (1, 3, 2):
        arrived(arecv.at[(x + 4 - d) % 4], a_r.at[d])

    order = [(zh + 2) % 4, (zh + 1) % 4, (zh + 3) % 4, 4, zh]

    def rows_of(p):
        return pl.ds(pl.multiple_of(p * LINE, 16), LINE)

    for j in range(NK):
        mine = jnp.concatenate([arecv[s, order[j], 0:OWN, :] for s in range(4)], axis=0)
        xs[x, j, rows_of(zl), :] = mine

    def line_copy(j, side, t):
        step = 1 if side == 0 else -1
        block = xs.at[x, j, rows_of(zl - step * (t - 1))]
        return remote(block, block, l_s.at[side, j, t], l_r.at[side, j, t], at_line(step))

    def line_sends(side, t):
        if side == 0:
            return jnp.logical_and(zl - (t - 1) >= 0, zl < NZ - 1)
        return jnp.logical_and(zl + (t - 1) <= NZ - 1, zl > 0)

    def line_gets(side, t):
        return zl - t >= 0 if side == 0 else zl + t <= NZ - 1

    def wave(w_at):
        for j in range(NK):
            t = w_at - 2 * j
            if t < 0 or t > NZ - 1:
                continue
            for side in range(2):
                if t >= 1:
                    @pl.when(line_gets(side, t))
                    def _():
                        step = 1 if side == 0 else -1
                        arrived(xs.at[x, j, rows_of(zl - step * t)], l_r.at[side, j, t])

                if t + 1 <= NZ - 1:
                    @pl.when(line_sends(side, t + 1))
                    def _():
                        line_copy(j, side, t + 1).start()

    def permute(q):
        if q == 0:
            loads[2].wait()
        for k in range(NK):
            lo, hi = tile_columns(lambda at, n: w[:, q * QUARTER + at : q * QUARTER + at + n], k)
            wp[q, k, :, 0:128] = lo
            wp[q, k, :, 128:256] = hi

    def partial(q, j):
        value = jnp.dot(ht[...], xs[q, j], preferred_element_type=F32)
        lo, hi = value[:, 0:128], value[:, 128:256]
        pm[q, j] = jnp.where(core == 0, lo, hi)
        csend[q, j] = jnp.where(core == 0, hi, lo).astype(BF)
        send(csend.at[q, j], crecv.at[q, j], c_s.at[q, j], c_r.at[q, j], other)

    left, right, far = (x + 3) % 4, (x + 1) % 4, (x + 2) % 4
    up_half, down_half = pl.ds(0, TOK // 2), pl.ds(TOK // 2, TOK // 2)

    def op_a(j):
        block = xs.at[x, j]
        send(block, block, x_s.at[0, j], x_r.at[0, j], at_x(1))
        send(block, block, x_s.at[1, j], x_r.at[1, j], at_x(3))
        partial(x, j)

    def op_d(j):
        arrived(xs.at[left, j], x_r.at[0, j])
        block = xs.at[left, j, up_half]
        send(block, block, x_s.at[2, j], x_r.at[2, j], at_x(1))
        arrived(xs.at[right, j], x_r.at[1, j])
        block = xs.at[right, j, down_half]
        send(block, block, x_s.at[3, j], x_r.at[3, j], at_x(3))
        partial(left, j)
        partial(right, j)

    def op_e(j):
        arrived(xs.at[far, j, up_half], x_r.at[2, j])
        arrived(xs.at[far, j, down_half], x_r.at[3, j])
        partial(far, j)

    lo_r, hi_r = pl.ds(0, HALF), pl.ds(HALF, HALF)
    y_far, y_next, y_prev = (y + 2) % 4, (y + 1) % 4, (y + 3) % 4

    def op_f(j):
        for q in range(4):
            arrived(crecv.at[q, j], c_r.at[q, j])
        y1s[j] = (pm[y_far, j] + crecv[y_far, j].astype(F32)).astype(BF)
        send(y1s.at[j, lo_r], y1r.at[j, lo_r], y_s.at[0, j], y_r.at[0, j], at_y(1))
        send(y1s.at[j, hi_r], y1r.at[j, hi_r], y_s.at[1, j], y_r.at[1, j], at_y(3))
        y2s[0, j, hi_r] = (pm[y_next, j, hi_r] + crecv[y_next, j, hi_r].astype(F32)).astype(BF)
        send(y2s.at[0, j, hi_r], y2r.at[0, j, hi_r], y_s.at[2, j], y_r.at[2, j], at_y(1))
        y2s[1, j, lo_r] = (pm[y_prev, j, lo_r] + crecv[y_prev, j, lo_r].astype(F32)).astype(BF)
        send(y2s.at[1, j, lo_r], y2r.at[1, j, lo_r], y_s.at[3, j], y_r.at[3, j], at_y(3))

    def op_g(j):
        arrived(y1r.at[j, lo_r], y_r.at[0, j])
        y2s[0, j, lo_r] = (
            pm[y_next, j, lo_r] + crecv[y_next, j, lo_r].astype(F32) + y1r[j, lo_r].astype(F32)
        ).astype(BF)
        send(y2s.at[0, j, lo_r], y2r.at[0, j, lo_r], y_s.at[4, j], y_r.at[4, j], at_y(1))
        arrived(y1r.at[j, hi_r], y_r.at[1, j])
        y2s[1, j, hi_r] = (
            pm[y_prev, j, hi_r] + crecv[y_prev, j, hi_r].astype(F32) + y1r[j, hi_r].astype(F32)
        ).astype(BF)
        send(y2s.at[1, j, hi_r], y2r.at[1, j, hi_r], y_s.at[5, j], y_r.at[5, j], at_y(3))

    def reduced(j):
        arrived(y2r.at[0, j, hi_r], y_r.at[2, j])
        arrived(y2r.at[1, j, lo_r], y_r.at[3, j])
        arrived(y2r.at[0, j, lo_r], y_r.at[4, j])
        arrived(y2r.at[1, j, hi_r], y_r.at[5, j])
        return (
            pm[y, j] + crecv[y, j].astype(F32) + y2r[0, j].astype(F32) + y2r[1, j].astype(F32)
        )

    z_far, z_next, z_prev = (zh + 2) % 4, (zh + 1) % 4, (zh + 3) % 4

    def op_h(j):
        total = reduced(j)
        if j == 0:
            z1s[...] = total.astype(BF)
            send(z1s.at[lo_r], z1r.at[lo_r], z_s.at[0], z_r.at[0], at_z(1))
            send(z1s.at[hi_r], z1r.at[hi_r], z_s.at[1], z_r.at[1], at_z(3))
        elif j == 1:
            zf[0] = total
            z2s[0, hi_r] = total[HALF:].astype(BF)
            send(z2s.at[0, hi_r], z2r.at[0, hi_r], z_s.at[2], z_r.at[2], at_z(1))
        elif j == 2:
            zf[1] = total
            z2s[1, lo_r] = total[:HALF].astype(BF)
            send(z2s.at[1, lo_r], z2r.at[1, lo_r], z_s.at[3], z_r.at[3], at_z(3))
        elif j == 3:
            for o in range(4):
                pr[o] = jnp.concatenate(
                    [total[RR * n : RR * n + RR, 32 * o : 32 * o + 32] for n in range(4)], axis=1
                )
            q1s[...] = pr[z_far].astype(BF)
            send(q1s.at[c0], q1r.at[c0], z_s.at[6], z_r.at[6], at_z(1))
            send(q1s.at[c1], q1r.at[c1], z_s.at[7], z_r.at[7], at_z(3))
            q2s[0, c1] = pr[z_next, c1].astype(BF)
            send(q2s.at[0, c1], q2r.at[0, c1], z_s.at[8], z_r.at[8], at_z(1))
            q2s[1, c0] = pr[z_prev, c0].astype(BF)
            send(q2s.at[1, c0], q2r.at[1, c0], z_s.at[9], z_r.at[9], at_z(3))
        else:
            zf[2] = total

    c0, c1 = pl.ds(0, R0), pl.ds(R0, RR - R0)

    def z_clockwise():
        arrived(z1r.at[lo_r], z_r.at[0])
        z2s[0, lo_r] = (zf[0, lo_r] + z1r[lo_r].astype(F32)).astype(BF)
        send(z2s.at[0, lo_r], z2r.at[0, lo_r], z_s.at[4], z_r.at[4], at_z(1))

    def z_back():
        arrived(z1r.at[hi_r], z_r.at[1])
        z2s[1, hi_r] = (zf[1, hi_r] + z1r[hi_r].astype(F32)).astype(BF)
        send(z2s.at[1, hi_r], z2r.at[1, hi_r], z_s.at[5], z_r.at[5], at_z(3))

    def z_rest():
        arrived(q1r.at[c0], z_r.at[6])
        q2s[0, c0] = (pr[z_next, c0] + q1r[c0].astype(F32)).astype(BF)
        send(q2s.at[0, c0], q2r.at[0, c0], z_s.at[10], z_r.at[10], at_z(1))
        arrived(q1r.at[c1], z_r.at[7])
        q2s[1, c1] = (pr[z_prev, c1] + q1r[c1].astype(F32)).astype(BF)
        send(q2s.at[1, c1], q2r.at[1, c1], z_s.at[11], z_r.at[11], at_z(3))

    def back(j):
        value = None
        for q in range(4):
            term = lax.dot_general(
                xs[q, j], wp[q, order[j]], (((1,), (1,)), ((), ())), preferred_element_type=F32
            )
            value = term if value is None else value + term
        if j == 0:
            bg[...] = value
        else:
            bg[...] += value

    wave(0)
    for n in range(4):
        wave(n + 1)
        permute(n)
    wave(5)
    wave(6)
    wave(7)
    op_a(0)
    wave(8)
    wave(9)
    wave(10)
    op_d(0)
    op_a(1)
    wave(11)
    op_a(2)
    wave(12)
    op_e(0)
    wave(13)
    op_f(0)
    op_d(1)
    wave(14)
    op_a(3)
    op_g(0)
    wave(15)
    op_e(1)
    op_h(0)
    op_f(1)
    op_d(2)
    op_a(4)
    op_g(1)
    op_e(2)
    op_h(1)
    op_f(2)
    op_d(3)
    op_g(2)
    op_e(3)
    op_h(2)
    op_f(3)
    z_clockwise()
    op_d(4)
    op_g(3)
    op_e(4)
    z_back()
    op_h(3)
    op_f(4)
    back(0)
    op_g(4)
    back(1)
    op_h(4)
    z_rest()
    back(2)
    back(3)
    back(4)

    gate_wide = gate[...].astype(F32)
    up_wide = up[...].astype(F32)
    sig = jax.nn.sigmoid(gate_wide)
    back_grad = bg[...]
    ug[...] = (back_grad * (gate_wide * sig)).astype(BF)
    gg[...] = (back_grad * up_wide * sig * (1.0 + gate_wide * (1.0 - sig))).astype(BF)

    factor = jnp.float32(float(TOK * 32) ** -0.5)
    for n in (2, 4):
        arrived(z2r.at[0, hi_r if n == 2 else lo_r], z_r.at[n])
        arrived(z2r.at[1, lo_r if n == 2 else hi_r], z_r.at[n + 1])
    wg[:, 0:128] = (zf[2] + z2r[0].astype(F32) + z2r[1].astype(F32)) * factor
    arrived(q2r.at[0, c1], z_r.at[8])
    arrived(q2r.at[1, c0], z_r.at[9])
    arrived(q2r.at[0, c0], z_r.at[10])
    arrived(q2r.at[1, c1], z_r.at[11])
    rest = (pr[zh] + q2r[0].astype(F32) + q2r[1].astype(F32)) * factor
    for n in range(4):
        wg[RR * n : RR * n + RR, 128:WIDE] = rest[:, 32 * n : 32 * n + 32]

    for copy in drains:
        copy.wait_send()
    for j in range(NK):
        for side in range(2):
            for t in range(1, NZ):
                @pl.when(line_sends(side, t))
                def _():
                    line_copy(j, side, t).wait_send()


def per_device(out_grad, gate_pre, up_pre, down_weight):
    vmem, dma = pltpu.VMEM, pltpu.SemaphoreType.DMA
    anywhere = pl.BlockSpec(memory_space=pl.ANY)
    local = pl.BlockSpec(memory_space=pltpu.VMEM)
    return pl.pallas_call(
        kernel,
        out_shape=(
            jax.ShapeDtypeStruct((TOK, FFL), BF),
            jax.ShapeDtypeStruct((TOK, FFL), BF),
            jax.ShapeDtypeStruct((FFL, WIDE), F32),
        ),
        in_specs=[local, anywhere, anywhere, anywhere],
        out_specs=(local, local, local),
        scratch_shapes=[
            vmem((TOK, FFL), BF),
            vmem((TOK, FFL), BF),
            vmem((FFL, 4 * QUARTER), BF),
            vmem((4, NK, FFL, 256), BF),
            vmem((FFL, TOK), BF),
            vmem((4, NK, TOK, 256), BF),
            vmem((4, NK, 16, 256), BF),
            vmem((4, NK, 16, 256), BF),
            vmem((TOK, FFL), F32),
            vmem((4, NK, FFL, 128), F32),
            vmem((4, NK, FFL, 128), BF),
            vmem((4, NK, FFL, 128), BF),
            vmem((NK, FFL, 128), BF),
            vmem((NK, FFL, 128), BF),
            vmem((2, NK, FFL, 128), BF),
            vmem((2, NK, FFL, 128), BF),
            vmem((FFL, 128), BF),
            vmem((FFL, 128), BF),
            vmem((2, FFL, 128), BF),
            vmem((2, FFL, 128), BF),
            vmem((3, FFL, 128), F32),
            vmem((4, RR, 128), F32),
            vmem((RR, 128), BF),
            vmem((RR, 128), BF),
            vmem((2, RR, 128), BF),
            vmem((2, RR, 128), BF),
            dma((3,)),
            dma((4,)),
            dma((4,)),
            dma((2, NK, NZ)),
            dma((2, NK, NZ)),
            dma((4, NK)),
            dma((4, NK)),
            dma((4, NK)),
            dma((4, NK)),
            dma((6, NK)),
            dma((6, NK)),
            dma((12,)),
            dma((12,)),
        ],
        compiler_params=pltpu.CompilerParams(
            collective_id=0, has_side_effects=True, vmem_limit_bytes=56 * 2**20
        ),
        cost_estimate=pl.CostEstimate(
            flops=4 * TOK * FFL * 4 * QUARTER, bytes_accessed=7 * 2**20, transcendentals=2 * TOK * FFL
        ),
    )(out_grad, gate_pre, up_pre, down_weight)


def solution(mesh):
    placed = (P(("dp", "tensor"), None), P("dp", "tensor"), P("dp", "tensor"), P("tensor", None))
    return jax.shard_map(
        per_device,
        mesh=mesh,
        in_specs=placed,
        out_specs=(P("dp", "tensor"), P("dp", "tensor"), P("tensor", "dp")),
        check_vma=False,
    )
```

```python
import functools

import jax
import jax.numpy as jnp
from jax import lax
from jax.experimental import pallas as pl
from jax.experimental.pallas import tpu as pltpu
from jax.sharding import PartitionSpec as P

MESH = pl.DeviceIdType.MESH
BF = jnp.bfloat16
F32 = jnp.float32

NX = 4
NZ = 8
NK = 5
TOK = 384
OWN = 12
LINE = 48
FFL = 448
HALF = 224
QUARTER = 1280
WIDE = 160
R0 = 64
RR = 112
NB = 1


def tile_columns(load, k):
    sides = []
    for c in range(2):
        if k < 4:
            at = k * 2 * WIDE + c * WIDE
            sides.append(load(at, 128))
        else:
            sides.append(
                jnp.concatenate([load(z * 2 * WIDE + c * WIDE + 128, 32) for z in range(4)], axis=1)
            )
    return sides


def kernel(
    og, gate_hbm, up_hbm, w_hbm,
    gg, ug, wg,
    gate, up, w, wp, ht, xs, asend, arecv, bg, pm, csend, crecv,
    ys, yr, z1s, z1r, z2s, z2r, zf, pr, q1s, q1r, q2s, q2r,
    lsem, a_s, a_r, d_s, d_r, l_s, l_r, b_s, b_r, x_s, x_r, c_s, c_r, y_s, y_r, z_s, z_r,
):
    dp = lax.axis_index("dp")
    tn = lax.axis_index("tensor")
    y, zh, core = dp // 8, (dp // 2) % 4, dp % 2
    zl, x = tn // 4, tn % 4

    def at_x(d):
        return (dp, zl * 4 + (x + d) % 4)

    def at_y(d):
        return (((y + d) % 4) * 8 + zh * 2 + core, tn)

    def at_z(d):
        return (y * 8 + ((zh + d) % 4) * 2 + core, tn)

    def at_line(d):
        return (dp, ((zl + d) % NZ) * 4 + x)

    other = (dp + 1 - 2 * core, tn)

    loads = [
        pltpu.make_async_copy(gate_hbm, gate, lsem.at[0]),
        pltpu.make_async_copy(up_hbm, up, lsem.at[1]),
        pltpu.make_async_copy(w_hbm, w, lsem.at[2]),
    ]
    for copy in loads:
        copy.start()

    barrier = pltpu.get_barrier_semaphore()

    def greet(device):
        pl.semaphore_signal(barrier, inc=1, device_id=device, device_id_type=MESH)

    for d in (1, 2, 3):
        greet(at_x(d))
        greet(at_y(d))
    for device in (other, at_z(1), at_z(3)):
        greet(device)
    for d in range(1, NZ):
        greet(at_line(d))

    def slot(k):
        if k == 4:
            return 3
        ahead = (k + 4 - zh) % 4
        return jnp.where(ahead == 2, 0, jnp.where(ahead == 1, 1, jnp.where(ahead == 3, 2, 4)))

    order = [(zh + 2) % 4, (zh + 1) % 4, (zh + 3) % 4, 4, zh]

    asend[...] = jnp.zeros_like(asend)
    for q in range(4):
        for k in range(NK):
            lo, hi = tile_columns(lambda at, n: og[:, q * QUARTER + at : q * QUARTER + at + n], k)
            asend[q, slot(k), 0:OWN, 0:128] = lo
            asend[q, slot(k), 0:OWN, 128:256] = hi
    pl.semaphore_wait(barrier, 9 + NZ - 1)

    drains = []

    def remote(src, dst, ss, rs, device):
        return pltpu.make_async_remote_copy(
            src_ref=src, dst_ref=dst, send_sem=ss, recv_sem=rs, device_id=device, device_id_type=MESH
        )

    def send(src, dst, ss, rs, device):
        copy = remote(src, dst, ss, rs, device)
        copy.start()
        drains.append(copy)

    def arrived(dst, rs):
        remote(dst, dst, rs, rs, other).wait_recv()

    def rows_of(p):
        return pl.ds(pl.multiple_of(p * LINE, 16), LINE)

    later = pl.ds(1, NK - 1)

    for d in (2, 1, 3):
        send(asend.at[(x + d) % 4, 0], arecv.at[x, 0], a_s.at[0, d], a_r.at[0, d], at_x(d))
    for d in (2, 1, 3):
        send(asend.at[(x + d) % 4, later], arecv.at[x, later], a_s.at[1, d], a_r.at[1, d], at_x(d))
    arecv[pl.ds(x, 1)] = asend[pl.ds(x, 1)]

    def own_rows(j):
        mine = jnp.concatenate([arecv[n, j, 0:OWN, :] for n in range(4)], axis=0)
        xs[x, j, rows_of(zl), :] = mine

    def to_ring(j, p):
        block = xs.at[x, j, rows_of(p)]
        for d in (2, 1, 3):
            remote(block, block, b_s.at[j, d], b_r.at[j, d], at_x(d)).start()

    for d in (1, 3, 2):
        arrived(arecv.at[(x + 4 - d) % 4, 0], a_r.at[0, d])
    own_rows(0)
    block = xs.at[x, 0, rows_of(zl)]
    for d in (4, 3, 5, 2, 6, 1, 7):
        remote(block, block, d_s.at[0], d_r.at[zl], at_line(d)).start()
    to_ring(0, zl)
    for d in (1, 3, 2):
        arrived(arecv.at[(x + 4 - d) % 4, later], a_r.at[1, d])
    for j in range(1, NK):
        own_rows(j)

    def line_copy(j, side, t):
        step = 1 if side == 0 else -1
        block = xs.at[x, j, rows_of(zl - step * (t - 1))]
        return remote(block, block, l_s.at[side, j, t], l_r.at[side, j, t], at_line(step))

    def line_sends(side, t):
        if side == 0:
            return jnp.logical_and(zl - (t - 1) >= 0, zl < NZ - 1)
        return jnp.logical_and(zl + (t - 1) <= NZ - 1, zl > 0)

    def line_gets(side, t):
        return zl - t >= 0 if side == 0 else zl + t <= NZ - 1

    def wave(t):
        for j in range(1, NK):
            for side in range(2):
                step = 1 if side == 0 else -1
                if t >= 1:

                    @pl.when(line_gets(side, t))
                    def _():
                        arrived(xs.at[x, j, rows_of(zl - step * t)], l_r.at[side, j, t])

                if t + 1 <= NZ - 1:

                    @pl.when(line_sends(side, t + 1))
                    def _():
                        line_copy(j, side, t + 1).start()

                if t >= 1 and j <= NB:

                    @pl.when(line_gets(side, t))
                    def _():
                        to_ring(j, zl - step * t)

            if t == 0 and j <= NB:
                to_ring(j, zl)

    def direct(t):
        for side in range(2):
            step = 1 if side == 0 else -1

            @pl.when(line_gets(side, t))
            def _():
                p = zl - step * t
                arrived(xs.at[x, 0, rows_of(p)], d_r.at[p])
                to_ring(0, p)

    def ring_in(j, d):
        q = (x + 4 - d) % 4
        arrived(xs.at[q, j], b_r.at[j, d])
        partial(q, j)

    def permute(q):
        if q == 0:
            loads[2].wait()
        for k in range(NK):
            lo, hi = tile_columns(lambda at, n: w[:, q * QUARTER + at : q * QUARTER + at + n], k)
            wp[q, k, :, 0:128] = lo
            wp[q, k, :, 128:256] = hi

    def partial(q, j):
        value = jnp.dot(ht[...], xs[q, j], preferred_element_type=F32)
        lo, hi = value[:, 0:128], value[:, 128:256]
        pm[q, j] = jnp.where(core == 0, lo, hi)
        csend[q, j] = jnp.where(core == 0, hi, lo).astype(BF)
        send(csend.at[q, j], crecv.at[q, j], c_s.at[q, j], c_r.at[q, j], other)

    left, right, far = (x + 3) % 4, (x + 1) % 4, (x + 2) % 4
    up_half, down_half = pl.ds(0, TOK // 2), pl.ds(TOK // 2, TOK // 2)

    def op_a(j):
        block = xs.at[x, j]
        send(block, block, x_s.at[0, j], x_r.at[0, j], at_x(1))
        send(block, block, x_s.at[1, j], x_r.at[1, j], at_x(3))
        partial(x, j)

    def op_d(j):
        arrived(xs.at[left, j], x_r.at[0, j])
        block = xs.at[left, j, up_half]
        send(block, block, x_s.at[2, j], x_r.at[2, j], at_x(1))
        arrived(xs.at[right, j], x_r.at[1, j])
        block = xs.at[right, j, down_half]
        send(block, block, x_s.at[3, j], x_r.at[3, j], at_x(3))
        partial(left, j)
        partial(right, j)

    def op_e(j):
        arrived(xs.at[far, j, up_half], x_r.at[2, j])
        arrived(xs.at[far, j, down_half], x_r.at[3, j])
        partial(far, j)

    lo_r, hi_r = pl.ds(0, HALF), pl.ds(HALF, HALF)

    def op_f(j):
        for q in range(4):
            arrived(crecv.at[q, j], c_r.at[q, j])
        for d in (2, 1, 3):
            q = (y + d) % 4
            ys[d - 1, j] = (pm[q, j] + crecv[q, j].astype(F32)).astype(BF)
            send(ys.at[d - 1, j], yr.at[d - 1, j], y_s.at[d - 1, j], y_r.at[d - 1, j], at_y(d))

    def reduced(j):
        total = pm[y, j] + crecv[y, j].astype(F32)
        for d in (1, 3, 2):
            arrived(yr.at[d - 1, j], y_r.at[d - 1, j])
            total = total + yr[d - 1, j].astype(F32)
        return total

    z_far, z_next, z_prev = (zh + 2) % 4, (zh + 1) % 4, (zh + 3) % 4

    def op_h(j):
        total = reduced(j)
        if j == 0:
            z1s[...] = total.astype(BF)
            send(z1s.at[lo_r], z1r.at[lo_r], z_s.at[0], z_r.at[0], at_z(1))
            send(z1s.at[hi_r], z1r.at[hi_r], z_s.at[1], z_r.at[1], at_z(3))
        elif j == 1:
            zf[0] = total
            z2s[0, hi_r] = total[HALF:].astype(BF)
            send(z2s.at[0, hi_r], z2r.at[0, hi_r], z_s.at[2], z_r.at[2], at_z(1))
        elif j == 2:
            zf[1] = total
            z2s[1, lo_r] = total[:HALF].astype(BF)
            send(z2s.at[1, lo_r], z2r.at[1, lo_r], z_s.at[3], z_r.at[3], at_z(3))
        elif j == 3:
            for o in range(4):
                pr[o] = jnp.concatenate(
                    [total[RR * n : RR * n + RR, 32 * o : 32 * o + 32] for n in range(4)], axis=1
                )
            q1s[...] = pr[z_far].astype(BF)
            send(q1s.at[c0], q1r.at[c0], z_s.at[6], z_r.at[6], at_z(1))
            send(q1s.at[c1], q1r.at[c1], z_s.at[7], z_r.at[7], at_z(3))
            q2s[0, c1] = pr[z_next, c1].astype(BF)
            send(q2s.at[0, c1], q2r.at[0, c1], z_s.at[8], z_r.at[8], at_z(1))
            q2s[1, c0] = pr[z_prev, c0].astype(BF)
            send(q2s.at[1, c0], q2r.at[1, c0], z_s.at[9], z_r.at[9], at_z(3))
        else:
            zf[2] = total

    c0, c1 = pl.ds(0, R0), pl.ds(R0, RR - R0)

    def z_clockwise():
        arrived(z1r.at[lo_r], z_r.at[0])
        z2s[0, lo_r] = (zf[0, lo_r] + z1r[lo_r].astype(F32)).astype(BF)
        send(z2s.at[0, lo_r], z2r.at[0, lo_r], z_s.at[4], z_r.at[4], at_z(1))

    def z_back():
        arrived(z1r.at[hi_r], z_r.at[1])
        z2s[1, hi_r] = (zf[1, hi_r] + z1r[hi_r].astype(F32)).astype(BF)
        send(z2s.at[1, hi_r], z2r.at[1, hi_r], z_s.at[5], z_r.at[5], at_z(3))

    def z_rest():
        arrived(q1r.at[c0], z_r.at[6])
        q2s[0, c0] = (pr[z_next, c0] + q1r[c0].astype(F32)).astype(BF)
        send(q2s.at[0, c0], q2r.at[0, c0], z_s.at[10], z_r.at[10], at_z(1))
        arrived(q1r.at[c1], z_r.at[7])
        q2s[1, c1] = (pr[z_prev, c1] + q1r[c1].astype(F32)).astype(BF)
        send(q2s.at[1, c1], q2r.at[1, c1], z_s.at[11], z_r.at[11], at_z(3))

    def back(j):
        value = None
        for q in range(4):
            term = lax.dot_general(
                wp[q, order[j]], xs[q, j], (((1,), (1,)), ((), ())), preferred_element_type=F32
            )
            value = term if value is None else value + term
        if j == 0:
            bg[...] = value
        else:
            bg[...] += value

    wave(0)
    loads[0].wait()
    loads[1].wait()
    g = gate[...].astype(F32)
    ht[...] = (g * jax.nn.sigmoid(g) * up[...].astype(F32)).astype(BF)
    direct(1)
    direct(2)
    wave(1)
    direct(3)
    direct(4)
    wave(2)
    direct(5)
    direct(6)
    direct(7)
    wave(3)
    partial(x, 0)
    wave(4)
    ring_in(0, 1)
    ring_in(0, 3)
    wave(5)
    ring_in(0, 2)
    wave(6)
    op_f(0)
    wave(7)
    op_a(2)
    partial(x, 1)
    ring_in(1, 1)
    ring_in(1, 3)
    op_a(3)
    ring_in(1, 2)
    op_h(0)
    op_f(1)
    op_d(2)
    op_a(4)
    op_e(2)
    op_h(1)
    op_f(2)
    op_d(3)
    op_e(3)
    op_h(2)
    op_f(3)
    z_clockwise()
    z_back()
    op_d(4)
    op_h(3)
    op_e(4)
    op_f(4)
    permute(0)
    permute(1)
    z_rest()
    op_h(4)
    permute(2)
    permute(3)
    back(0)
    back(1)
    back(2)
    back(3)
    back(4)

    gate_wide = gate[...].astype(F32)
    up_wide = up[...].astype(F32)
    sig = jax.nn.sigmoid(gate_wide)
    back_grad = bg[...]
    ug[...] = (back_grad * (gate_wide * sig)).astype(BF)
    gg[...] = (back_grad * up_wide * sig * (1.0 + gate_wide * (1.0 - sig))).astype(BF)

    factor = jnp.float32(float(TOK * 32) ** -0.5)
    for n in (2, 4):
        arrived(z2r.at[0, hi_r if n == 2 else lo_r], z_r.at[n])
        arrived(z2r.at[1, lo_r if n == 2 else hi_r], z_r.at[n + 1])
    wg[0:128] = ((zf[2] + z2r[0].astype(F32) + z2r[1].astype(F32)) * factor).T
    arrived(q2r.at[0, c1], z_r.at[8])
    arrived(q2r.at[1, c0], z_r.at[9])
    arrived(q2r.at[0, c0], z_r.at[10])
    arrived(q2r.at[1, c1], z_r.at[11])
    rest = ((pr[zh] + q2r[0].astype(F32) + q2r[1].astype(F32)) * factor).T
    wg[128:WIDE] = jnp.concatenate([rest[32 * n : 32 * n + 32] for n in range(4)], axis=1)

    for copy in drains:
        copy.wait_send()
    others = xs.at[0, 0, pl.ds(0, (NZ - 1) * LINE)]
    remote(others, others, d_s.at[0], d_s.at[0], other).wait_send()
    for j in range(NB + 1):
        for d in (1, 2, 3):
            remote(xs.at[x, j], xs.at[x, j], b_s.at[j, d], b_s.at[j, d], other).wait_send()
    for j in range(1, NK):
        for side in range(2):
            for t in range(1, NZ):

                @pl.when(line_sends(side, t))
                def _():
                    line_copy(j, side, t).wait_send()


def per_device(out_grad, gate_pre, up_pre, down_weight):
    vmem, dma = pltpu.VMEM, pltpu.SemaphoreType.DMA
    anywhere = pl.BlockSpec(memory_space=pl.ANY)
    local = pl.BlockSpec(memory_space=pltpu.VMEM)
    gate_grad, up_grad, weight_grad = pl.pallas_call(
        kernel,
        out_shape=(
            jax.ShapeDtypeStruct((FFL, TOK), BF),
            jax.ShapeDtypeStruct((FFL, TOK), BF),
            jax.ShapeDtypeStruct((WIDE, FFL), F32),
        ),
        in_specs=[local, anywhere, anywhere, anywhere],
        out_specs=(local, local, local),
        scratch_shapes=[
            vmem((FFL, TOK), BF),
            vmem((FFL, TOK), BF),
            vmem((FFL, 4 * QUARTER), BF),
            vmem((4, NK, FFL, 256), BF),
            vmem((FFL, TOK), BF),
            vmem((4, NK, TOK, 256), BF),
            vmem((4, NK, 16, 256), BF),
            vmem((4, NK, 16, 256), BF),
            vmem((FFL, TOK), F32),
            vmem((4, NK, FFL, 128), F32),
            vmem((4, NK, FFL, 128), BF),
            vmem((4, NK, FFL, 128), BF),
            vmem((3, NK, FFL, 128), BF),
            vmem((3, NK, FFL, 128), BF),
            vmem((FFL, 128), BF),
            vmem((FFL, 128), BF),
            vmem((2, FFL, 128), BF),
            vmem((2, FFL, 128), BF),
            vmem((3, FFL, 128), F32),
            vmem((4, RR, 128), F32),
            vmem((RR, 128), BF),
            vmem((RR, 128), BF),
            vmem((2, RR, 128), BF),
            vmem((2, RR, 128), BF),
            dma((3,)),
            dma((2, 4)),
            dma((2, 4)),
            dma((1,)),
            dma((NZ,)),
            dma((2, NK, NZ)),
            dma((2, NK, NZ)),
            dma((NB + 1, 4)),
            dma((NB + 1, 4)),
            dma((4, NK)),
            dma((4, NK)),
            dma((4, NK)),
            dma((4, NK)),
            dma((3, NK)),
            dma((3, NK)),
            dma((12,)),
            dma((12,)),
        ],
        compiler_params=pltpu.CompilerParams(
            collective_id=0, has_side_effects=True, vmem_limit_bytes=56 * 2**20
        ),
        cost_estimate=pl.CostEstimate(
            flops=4 * TOK * FFL * 4 * QUARTER, bytes_accessed=7 * 2**20, transcendentals=2 * TOK * FFL
        ),
    )(out_grad, gate_pre.T, up_pre.T, down_weight)
    return gate_grad.T, up_grad.T, weight_grad.T


def solution(mesh):
    placed = (P(("dp", "tensor"), None), P("dp", "tensor"), P("dp", "tensor"), P("tensor", None))
    return jax.shard_map(
        per_device,
        mesh=mesh,
        in_specs=placed,
        out_specs=(P("dp", "tensor"), P("dp", "tensor"), P("tensor", "dp")),
        check_vma=False,
    )
```

```python
import functools

import jax
import jax.numpy as jnp
from jax import lax
from jax.experimental import pallas as pl
from jax.experimental.pallas import tpu as pltpu
from jax.sharding import PartitionSpec as P

MESH = pl.DeviceIdType.MESH
BF = jnp.bfloat16
F32 = jnp.float32

NX = 4
NZ = 8
NK = 5
TOK = 384
OWN = 12
LINE = 48
FFL = 448
HALF = 224
QUARTER = 1280
WIDE = 160
R0 = 64
RR = 112
NB = 2
NS = 2


def tile_columns(load, k):
    sides = []
    for c in range(2):
        if k < 4:
            at = k * 2 * WIDE + c * WIDE
            sides.append(load(at, 128))
        else:
            sides.append(
                jnp.concatenate([load(z * 2 * WIDE + c * WIDE + 128, 32) for z in range(4)], axis=1)
            )
    return sides


def kernel(
    og, gate_hbm, up_hbm, w_hbm,
    gg, ug, wg,
    gate, up, w, wp, ht, xs, asend, arecv, bg, pm, csend, crecv,
    ys, yr, z1s, z1r, z2s, z2r, zf, pr, q1s, q1r, q2s, q2r,
    lsem, a_s, a_r, d_s, d_r, l_s, l_r, b_s, b_r, x_s, x_r, c_s, c_r, y_s, y_r, z_s, z_r,
):
    dp = lax.axis_index("dp")
    tn = lax.axis_index("tensor")
    y, zh, core = dp // 8, (dp // 2) % 4, dp % 2
    zl, x = tn // 4, tn % 4

    def at_x(d):
        return (dp, zl * 4 + (x + d) % 4)

    def at_y(d):
        return (((y + d) % 4) * 8 + zh * 2 + core, tn)

    def at_z(d):
        return (y * 8 + ((zh + d) % 4) * 2 + core, tn)

    def at_line(d):
        return (dp, ((zl + d) % NZ) * 4 + x)

    other = (dp + 1 - 2 * core, tn)

    loads = [
        pltpu.make_async_copy(gate_hbm, gate, lsem.at[0]),
        pltpu.make_async_copy(up_hbm, up, lsem.at[1]),
        pltpu.make_async_copy(w_hbm, w, lsem.at[2]),
    ]
    for copy in loads:
        copy.start()

    barrier = pltpu.get_barrier_semaphore()

    def greet(device):
        pl.semaphore_signal(barrier, inc=1, device_id=device, device_id_type=MESH)

    for d in (1, 2, 3):
        greet(at_x(d))
        greet(at_y(d))
    for device in (other, at_z(1), at_z(3)):
        greet(device)
    for d in range(1, NZ):
        greet(at_line(d))

    def slot(k):
        if k == 4:
            return 3
        ahead = (k + 4 - zh) % 4
        return jnp.where(ahead == 2, 0, jnp.where(ahead == 1, 1, jnp.where(ahead == 3, 2, 4)))

    order = [(zh + 2) % 4, (zh + 1) % 4, (zh + 3) % 4, 4, zh]

    asend[...] = jnp.zeros_like(asend)
    for q in range(4):
        for k in range(NK):
            lo, hi = tile_columns(lambda at, n: og[:, q * QUARTER + at : q * QUARTER + at + n], k)
            asend[q, slot(k), 0:OWN, 0:128] = lo
            asend[q, slot(k), 0:OWN, 128:256] = hi
    pl.semaphore_wait(barrier, 9 + NZ - 1)

    drains = []

    def remote(src, dst, ss, rs, device):
        return pltpu.make_async_remote_copy(
            src_ref=src, dst_ref=dst, send_sem=ss, recv_sem=rs, device_id=device, device_id_type=MESH
        )

    def send(src, dst, ss, rs, device):
        copy = remote(src, dst, ss, rs, device)
        copy.start()
        drains.append(copy)

    def arrived(dst, rs):
        remote(dst, dst, rs, rs, other).wait_recv()

    def rows_of(p):
        return pl.ds(pl.multiple_of(p * LINE, 16), LINE)

    later = pl.ds(1, NK - 1)

    for d in (2, 1, 3):
        send(asend.at[(x + d) % 4, 0], arecv.at[x, 0], a_s.at[0, d], a_r.at[0, d], at_x(d))
    for d in (2, 1, 3):
        send(asend.at[(x + d) % 4, later], arecv.at[x, later], a_s.at[1, d], a_r.at[1, d], at_x(d))
    arecv[pl.ds(x, 1)] = asend[pl.ds(x, 1)]

    def own_rows(j):
        mine = jnp.concatenate([arecv[n, j, 0:OWN, :] for n in range(4)], axis=0)
        xs[x, j, rows_of(zl), :] = mine

    def to_ring(j, p):
        block = xs.at[x, j, rows_of(p)]
        if j == 0:
            for d in (2, 1, 3):
                remote(block, block, b_s.at[d], b_r.at[d], at_x(d)).start()
        else:
            remote(block, block, x_s.at[0, j], x_r.at[0, j], at_x(1)).start()
            remote(block, block, x_s.at[1, j], x_r.at[1, j], at_x(3)).start()

    for d in (1, 3, 2):
        arrived(arecv.at[(x + 4 - d) % 4, 0], a_r.at[0, d])
    own_rows(0)
    block = xs.at[x, 0, rows_of(zl)]
    for d in (4, 3, 5, 2, 6, 1, 7):
        remote(block, block, d_s.at[0], d_r.at[zl], at_line(d)).start()
    to_ring(0, zl)
    for d in (1, 3, 2):
        arrived(arecv.at[(x + 4 - d) % 4, later], a_r.at[1, d])
    for j in range(1, NK):
        own_rows(j)

    def line_copy(j, side, t):
        step = 1 if side == 0 else -1
        back, far = ((t - 1) // 2 * 2, 2 - t % 2) if j <= NS else (t - 1, 1)
        block = xs.at[x, j, rows_of(zl - step * back)]
        return remote(block, block, l_s.at[side, j, t], l_r.at[side, j, t], at_line(step * far))

    def line_sends(j, side, t):
        back, far = ((t - 1) // 2 * 2, 2 - t % 2) if j <= NS else (t - 1, 1)
        if side == 0:
            return jnp.logical_and(zl - back >= 0, zl + far <= NZ - 1)
        return jnp.logical_and(zl + back <= NZ - 1, zl - far >= 0)

    def line_gets(side, t):
        return zl - t >= 0 if side == 0 else zl + t <= NZ - 1

    def line_send(j, side, t):
        @pl.when(line_sends(j, side, t))
        def _():
            line_copy(j, side, t).start()

    def line_get(j, side, t):
        step = 1 if side == 0 else -1

        @pl.when(line_gets(side, t))
        def _():
            arrived(xs.at[x, j, rows_of(zl - step * t)], l_r.at[side, j, t])

    def line_ring(j, side, t):
        step = 1 if side == 0 else -1

        @pl.when(line_gets(side, t))
        def _():
            to_ring(j, zl - step * t)

    def wave(t):
        for j in range(1, NK):
            if j <= NS:
                if t > 4:
                    continue
                arrivals = [n for n in (2 * t, 2 * t - 1) if 1 <= n <= NZ - 1]
                relay, leave = 2 * t, [n for n in (2 * t + 2, 2 * t + 1) if n <= NZ - 1]
            else:
                arrivals = [t] if t >= 1 else []
                relay, leave = t, [t + 1] if t + 1 <= NZ - 1 else []
            for n in arrivals:
                for side in range(2):
                    line_get(j, side, n)
                    if n == relay:
                        for m in leave:
                            line_send(j, side, m)
                if j <= NB:
                    for side in range(2):
                        line_ring(j, side, n)
            if t == 0:
                for m in leave:
                    for side in range(2):
                        line_send(j, side, m)
                if j <= NB:
                    to_ring(j, zl)

    def direct(t):
        for side in range(2):
            step = 1 if side == 0 else -1

            @pl.when(line_gets(side, t))
            def _():
                p = zl - step * t
                arrived(xs.at[x, 0, rows_of(p)], d_r.at[p])
                to_ring(0, p)

    def ring_in(d):
        q = (x + 4 - d) % 4
        arrived(xs.at[q, 0], b_r.at[d])
        partial(q, 0)

    def permute(q):
        if q == 0:
            loads[2].wait()
        for k in range(NK):
            lo, hi = tile_columns(lambda at, n: w[:, q * QUARTER + at : q * QUARTER + at + n], k)
            wp[q, k, :, 0:128] = lo
            wp[q, k, :, 128:256] = hi

    def partial(q, j):
        value = jnp.dot(ht[...], xs[q, j], preferred_element_type=F32)
        lo, hi = value[:, 0:128], value[:, 128:256]
        pm[q, j] = jnp.where(core == 0, lo, hi)
        csend[q, j] = jnp.where(core == 0, hi, lo).astype(BF)
        send(csend.at[q, j], crecv.at[q, j], c_s.at[q, j], c_r.at[q, j], other)

    left, right, far = (x + 3) % 4, (x + 1) % 4, (x + 2) % 4
    up_half, down_half = pl.ds(0, TOK // 2), pl.ds(TOK // 2, TOK // 2)

    def op_a(j):
        block = xs.at[x, j]
        send(block, block, x_s.at[0, j], x_r.at[0, j], at_x(1))
        send(block, block, x_s.at[1, j], x_r.at[1, j], at_x(3))
        partial(x, j)

    def op_d(j):
        arrived(xs.at[left, j], x_r.at[0, j])
        block = xs.at[left, j, up_half]
        send(block, block, x_s.at[2, j], x_r.at[2, j], at_x(1))
        arrived(xs.at[right, j], x_r.at[1, j])
        block = xs.at[right, j, down_half]
        send(block, block, x_s.at[3, j], x_r.at[3, j], at_x(3))
        partial(left, j)
        partial(right, j)

    def op_e(j):
        arrived(xs.at[far, j, up_half], x_r.at[2, j])
        arrived(xs.at[far, j, down_half], x_r.at[3, j])
        partial(far, j)

    lo_r, hi_r = pl.ds(0, HALF), pl.ds(HALF, HALF)

    def op_f(j):
        for q in range(4):
            arrived(crecv.at[q, j], c_r.at[q, j])
        for d in (2, 1, 3):
            q = (y + d) % 4
            ys[d - 1, j] = (pm[q, j] + crecv[q, j].astype(F32)).astype(BF)
            send(ys.at[d - 1, j], yr.at[d - 1, j], y_s.at[d - 1, j], y_r.at[d - 1, j], at_y(d))

    def reduced(j):
        total = pm[y, j] + crecv[y, j].astype(F32)
        for d in (1, 3, 2):
            arrived(yr.at[d - 1, j], y_r.at[d - 1, j])
            total = total + yr[d - 1, j].astype(F32)
        return total

    z_far, z_next, z_prev = (zh + 2) % 4, (zh + 1) % 4, (zh + 3) % 4

    def op_h(j):
        total = reduced(j)
        if j == 0:
            z1s[...] = total.astype(BF)
            send(z1s.at[lo_r], z1r.at[lo_r], z_s.at[0], z_r.at[0], at_z(1))
            send(z1s.at[hi_r], z1r.at[hi_r], z_s.at[1], z_r.at[1], at_z(3))
        elif j == 1:
            zf[0] = total
            z2s[0, hi_r] = total[HALF:].astype(BF)
            send(z2s.at[0, hi_r], z2r.at[0, hi_r], z_s.at[2], z_r.at[2], at_z(1))
        elif j == 2:
            zf[1] = total
            z2s[1, lo_r] = total[:HALF].astype(BF)
            send(z2s.at[1, lo_r], z2r.at[1, lo_r], z_s.at[3], z_r.at[3], at_z(3))
        elif j == 3:
            for o in range(4):
                pr[o] = jnp.concatenate(
                    [total[RR * n : RR * n + RR, 32 * o : 32 * o + 32] for n in range(4)], axis=1
                )
            q1s[...] = pr[z_far].astype(BF)
            send(q1s.at[c0], q1r.at[c0], z_s.at[6], z_r.at[6], at_z(1))
            send(q1s.at[c1], q1r.at[c1], z_s.at[7], z_r.at[7], at_z(3))
            q2s[0, c1] = pr[z_next, c1].astype(BF)
            send(q2s.at[0, c1], q2r.at[0, c1], z_s.at[8], z_r.at[8], at_z(1))
            q2s[1, c0] = pr[z_prev, c0].astype(BF)
            send(q2s.at[1, c0], q2r.at[1, c0], z_s.at[9], z_r.at[9], at_z(3))
        else:
            zf[2] = total

    c0, c1 = pl.ds(0, R0), pl.ds(R0, RR - R0)

    def z_clockwise():
        arrived(z1r.at[lo_r], z_r.at[0])
        z2s[0, lo_r] = (zf[0, lo_r] + z1r[lo_r].astype(F32)).astype(BF)
        send(z2s.at[0, lo_r], z2r.at[0, lo_r], z_s.at[4], z_r.at[4], at_z(1))

    def z_back():
        arrived(z1r.at[hi_r], z_r.at[1])
        z2s[1, hi_r] = (zf[1, hi_r] + z1r[hi_r].astype(F32)).astype(BF)
        send(z2s.at[1, hi_r], z2r.at[1, hi_r], z_s.at[5], z_r.at[5], at_z(3))

    def z_rest():
        arrived(q1r.at[c0], z_r.at[6])
        q2s[0, c0] = (pr[z_next, c0] + q1r[c0].astype(F32)).astype(BF)
        send(q2s.at[0, c0], q2r.at[0, c0], z_s.at[10], z_r.at[10], at_z(1))
        arrived(q1r.at[c1], z_r.at[7])
        q2s[1, c1] = (pr[z_prev, c1] + q1r[c1].astype(F32)).astype(BF)
        send(q2s.at[1, c1], q2r.at[1, c1], z_s.at[11], z_r.at[11], at_z(3))

    def back(j):
        value = None
        for q in range(4):
            term = lax.dot_general(
                wp[q, order[j]], xs[q, j], (((1,), (1,)), ((), ())), preferred_element_type=F32
            )
            value = term if value is None else value + term
        if j == 0:
            bg[...] = value
        else:
            bg[...] += value

    wave(0)
    loads[0].wait()
    loads[1].wait()
    g = gate[...].astype(F32)
    ht[...] = (g * jax.nn.sigmoid(g) * up[...].astype(F32)).astype(BF)
    direct(1)
    direct(2)
    wave(1)
    direct(3)
    direct(4)
    direct(5)
    wave(2)
    direct(6)
    direct(7)
    partial(x, 0)
    wave(3)
    ring_in(1)
    ring_in(3)
    wave(4)
    partial(x, 1)
    ring_in(2)
    op_f(0)
    wave(5)
    op_d(1)
    wave(6)
    partial(x, 2)
    op_d(2)
    wave(7)
    op_a(3)
    op_e(1)
    op_a(4)
    op_h(0)
    op_f(1)
    op_e(2)
    op_f(2)
    op_h(1)
    op_d(3)
    op_h(2)
    op_e(3)
    z_clockwise()
    op_f(3)
    z_back()
    op_d(4)
    op_h(3)
    op_e(4)
    op_f(4)
    permute(0)
    permute(1)
    op_h(4)
    z_rest()
    permute(2)
    permute(3)
    back(0)
    back(1)
    back(2)
    back(3)
    back(4)

    gate_wide = gate[...].astype(F32)
    up_wide = up[...].astype(F32)
    sig = jax.nn.sigmoid(gate_wide)
    back_grad = bg[...]
    ug[...] = (back_grad * (gate_wide * sig)).astype(BF)
    gg[...] = (back_grad * up_wide * sig * (1.0 + gate_wide * (1.0 - sig))).astype(BF)

    factor = jnp.float32(float(TOK * 32) ** -0.5)
    for n in (2, 4):
        arrived(z2r.at[0, hi_r if n == 2 else lo_r], z_r.at[n])
        arrived(z2r.at[1, lo_r if n == 2 else hi_r], z_r.at[n + 1])
    wg[0:128] = ((zf[2] + z2r[0].astype(F32) + z2r[1].astype(F32)) * factor).T
    arrived(q2r.at[0, c1], z_r.at[8])
    arrived(q2r.at[1, c0], z_r.at[9])
    arrived(q2r.at[0, c0], z_r.at[10])
    arrived(q2r.at[1, c1], z_r.at[11])
    rest = ((pr[zh] + q2r[0].astype(F32) + q2r[1].astype(F32)) * factor).T
    wg[128:WIDE] = jnp.concatenate([rest[32 * n : 32 * n + 32] for n in range(4)], axis=1)

    for copy in drains:
        copy.wait_send()
    others = xs.at[0, 0, pl.ds(0, (NZ - 1) * LINE)]
    remote(others, others, d_s.at[0], d_s.at[0], other).wait_send()
    whole = xs.at[x, 0]
    for d in (1, 2, 3):
        remote(whole, whole, b_s.at[d], b_s.at[d], other).wait_send()
    for j in range(1, NB + 1):
        for n in (0, 1):
            remote(whole, whole, x_s.at[n, j], x_s.at[n, j], other).wait_send()
    for j in range(1, NK):
        for side in range(2):
            for t in range(1, NZ):

                @pl.when(line_sends(j, side, t))
                def _():
                    line_copy(j, side, t).wait_send()


def write_out(a, b, c, a_out, b_out, c_out):
    a_out[...] = a[...]
    b_out[...] = b[...]
    c_out[...] = c[...]


def per_device(out_grad, gate_pre, up_pre, down_weight):
    vmem, dma = pltpu.VMEM, pltpu.SemaphoreType.DMA
    anywhere = pl.BlockSpec(memory_space=pl.ANY)
    local = pl.BlockSpec(memory_space=pltpu.VMEM)
    sizes = (
        jax.ShapeDtypeStruct((FFL, TOK), BF),
        jax.ShapeDtypeStruct((FFL, TOK), BF),
        jax.ShapeDtypeStruct((WIDE, FFL), F32),
    )
    parts = pl.pallas_call(
        kernel,
        out_shape=sizes,
        in_specs=[local, anywhere, anywhere, anywhere],
        out_specs=(local, local, local),
        scratch_shapes=[
            vmem((FFL, TOK), BF),
            vmem((FFL, TOK), BF),
            vmem((FFL, 4 * QUARTER), BF),
            vmem((4, NK, FFL, 256), BF),
            vmem((FFL, TOK), BF),
            vmem((4, NK, TOK, 256), BF),
            vmem((4, NK, 16, 256), BF),
            vmem((4, NK, 16, 256), BF),
            vmem((FFL, TOK), F32),
            vmem((4, NK, FFL, 128), F32),
            vmem((4, NK, FFL, 128), BF),
            vmem((4, NK, FFL, 128), BF),
            vmem((3, NK, FFL, 128), BF),
            vmem((3, NK, FFL, 128), BF),
            vmem((FFL, 128), BF),
            vmem((FFL, 128), BF),
            vmem((2, FFL, 128), BF),
            vmem((2, FFL, 128), BF),
            vmem((3, FFL, 128), F32),
            vmem((4, RR, 128), F32),
            vmem((RR, 128), BF),
            vmem((RR, 128), BF),
            vmem((2, RR, 128), BF),
            vmem((2, RR, 128), BF),
            dma((3,)),
            dma((2, 4)),
            dma((2, 4)),
            dma((1,)),
            dma((NZ,)),
            dma((2, NK, NZ)),
            dma((2, NK, NZ)),
            dma((4,)),
            dma((4,)),
            dma((4, NK)),
            dma((4, NK)),
            dma((4, NK)),
            dma((4, NK)),
            dma((3, NK)),
            dma((3, NK)),
            dma((12,)),
            dma((12,)),
        ],
        compiler_params=pltpu.CompilerParams(
            collective_id=0, has_side_effects=True, vmem_limit_bytes=56 * 2**20
        ),
        cost_estimate=pl.CostEstimate(
            flops=4 * TOK * FFL * 4 * QUARTER, bytes_accessed=7 * 2**20, transcendentals=2 * TOK * FFL
        ),
    )(out_grad, gate_pre.T, up_pre.T, down_weight)
    gate_grad, up_grad, weight_grad = pl.pallas_call(
        write_out,
        out_shape=sizes,
        in_specs=[local] * 3,
        out_specs=(local,) * 3,
    )(*parts)
    return gate_grad.T, up_grad.T, weight_grad.T


def solution(mesh):
    placed = (P(("dp", "tensor"), None), P("dp", "tensor"), P("dp", "tensor"), P("tensor", None))
    return jax.shard_map(
        per_device,
        mesh=mesh,
        in_specs=placed,
        out_specs=(P("dp", "tensor"), P("dp", "tensor"), P("tensor", "dp")),
        check_vma=False,
    )
```

```python
import functools

import jax
import jax.numpy as jnp
from jax import lax
from jax.experimental import pallas as pl
from jax.experimental.pallas import tpu as pltpu
from jax.sharding import PartitionSpec as P

MESH = pl.DeviceIdType.MESH
BF = jnp.bfloat16
F32 = jnp.float32

NX = 4
NZ = 8
NK = 5
TOK = 384
OWN = 12
LINE = 48
FFL = 448
HALF = 224
QUARTER = 1280
WIDE = 160
R0 = 64
RR = 112
NB = 2
NS = 2


def tile_columns(load, k):
    sides = []
    for c in range(2):
        if k < 4:
            at = k * 2 * WIDE + c * WIDE
            sides.append(load(at, 128))
        else:
            sides.append(
                jnp.concatenate([load(z * 2 * WIDE + c * WIDE + 128, 32) for z in range(4)], axis=1)
            )
    return sides


def kernel(
    og, gate_hbm, up_hbm, w_hbm,
    gg, ug, wg,
    gate, up, w, wp, ht, xs, asend, arecv, bg, pm, csend, crecv,
    ys, yr, z1s, z1r, z2s, z2r, zf, pr, q1s, q1r, q2s, q2r,
    lsem, a_s, a_r, d_s, d_r, l_s, l_r, b_s, b_r, x_s, x_r, c_s, c_r, y_s, y_r, z_s, z_r,
):
    dp = lax.axis_index("dp")
    tn = lax.axis_index("tensor")
    y, zh, core = dp // 8, (dp // 2) % 4, dp % 2
    zl, x = tn // 4, tn % 4

    def at_x(d):
        return (dp, zl * 4 + (x + d) % 4)

    def at_y(d):
        return (((y + d) % 4) * 8 + zh * 2 + core, tn)

    def at_z(d):
        return (y * 8 + ((zh + d) % 4) * 2 + core, tn)

    def at_line(d):
        return (dp, ((zl + d) % NZ) * 4 + x)

    other = (dp + 1 - 2 * core, tn)

    loads = [
        pltpu.make_async_copy(gate_hbm, gate, lsem.at[0]),
        pltpu.make_async_copy(up_hbm, up, lsem.at[1]),
        pltpu.make_async_copy(w_hbm, w, lsem.at[2]),
    ]
    for copy in loads:
        copy.start()

    barrier = pltpu.get_barrier_semaphore()

    def greet(device):
        pl.semaphore_signal(barrier, inc=1, device_id=device, device_id_type=MESH)

    for d in (1, 2, 3):
        greet(at_x(d))
        greet(at_y(d))
    for device in (other, at_z(1), at_z(3)):
        greet(device)
    for d in range(1, NZ):
        greet(at_line(d))

    def slot(k):
        if k == 4:
            return 3
        ahead = (k + 4 - zh) % 4
        return jnp.where(ahead == 2, 0, jnp.where(ahead == 1, 1, jnp.where(ahead == 3, 2, 4)))

    order = [(zh + 2) % 4, (zh + 1) % 4, (zh + 3) % 4, 4, zh]

    asend[...] = jnp.zeros_like(asend)
    for q in range(4):
        for k in range(NK):
            lo, hi = tile_columns(lambda at, n: og[:, q * QUARTER + at : q * QUARTER + at + n], k)
            asend[q, slot(k), 0:OWN, 0:128] = lo
            asend[q, slot(k), 0:OWN, 128:256] = hi
    pl.semaphore_wait(barrier, 9 + NZ - 1)

    drains = []

    def remote(src, dst, ss, rs, device):
        return pltpu.make_async_remote_copy(
            src_ref=src, dst_ref=dst, send_sem=ss, recv_sem=rs, device_id=device, device_id_type=MESH
        )

    def send(src, dst, ss, rs, device):
        copy = remote(src, dst, ss, rs, device)
        copy.start()
        drains.append(copy)

    def arrived(dst, rs):
        remote(dst, dst, rs, rs, other).wait_recv()

    def rows_of(p):
        return pl.ds(pl.multiple_of(p * LINE, 16), LINE)

    later = pl.ds(1, NK - 1)

    for d in (2, 1, 3):
        send(asend.at[(x + d) % 4, 0], arecv.at[x, 0], a_s.at[0, d], a_r.at[0, d], at_x(d))
    for d in (2, 1, 3):
        send(asend.at[(x + d) % 4, later], arecv.at[x, later], a_s.at[1, d], a_r.at[1, d], at_x(d))
    arecv[pl.ds(x, 1)] = asend[pl.ds(x, 1)]

    def own_rows(j):
        mine = jnp.concatenate([arecv[n, j, 0:OWN, :] for n in range(4)], axis=0)
        xs[x, j, rows_of(zl), :] = mine

    def to_ring(j, p):
        block = xs.at[x, j, rows_of(p)]
        if j == 0:
            for d in (2, 1, 3):
                remote(block, block, b_s.at[d], b_r.at[d], at_x(d)).start()
        else:
            remote(block, block, x_s.at[0, j], x_r.at[0, j], at_x(1)).start()
            remote(block, block, x_s.at[1, j], x_r.at[1, j], at_x(3)).start()

    for d in (1, 3, 2):
        arrived(arecv.at[(x + 4 - d) % 4, 0], a_r.at[0, d])
    own_rows(0)
    block = xs.at[x, 0, rows_of(zl)]
    for d in (4, 3, 5, 2, 6, 1, 7):
        remote(block, block, d_s.at[0], d_r.at[zl], at_line(d)).start()
    to_ring(0, zl)
    for d in (1, 3, 2):
        arrived(arecv.at[(x + 4 - d) % 4, later], a_r.at[1, d])
    for j in range(1, NK):
        own_rows(j)

    def line_copy(j, side, t):
        step = 1 if side == 0 else -1
        back, far = ((t - 1) // 2 * 2, 2 - t % 2) if j <= NS else (t - 1, 1)
        block = xs.at[x, j, rows_of(zl - step * back)]
        return remote(block, block, l_s.at[side, j, t], l_r.at[side, j, t], at_line(step * far))

    def line_sends(j, side, t):
        back, far = ((t - 1) // 2 * 2, 2 - t % 2) if j <= NS else (t - 1, 1)
        if side == 0:
            return jnp.logical_and(zl - back >= 0, zl + far <= NZ - 1)
        return jnp.logical_and(zl + back <= NZ - 1, zl - far >= 0)

    def line_gets(side, t):
        return zl - t >= 0 if side == 0 else zl + t <= NZ - 1

    def line_send(j, side, t):
        @pl.when(line_sends(j, side, t))
        def _():
            line_copy(j, side, t).start()

    def line_get(j, side, t):
        step = 1 if side == 0 else -1

        @pl.when(line_gets(side, t))
        def _():
            arrived(xs.at[x, j, rows_of(zl - step * t)], l_r.at[side, j, t])

    def line_ring(j, side, t):
        step = 1 if side == 0 else -1

        @pl.when(line_gets(side, t))
        def _():
            to_ring(j, zl - step * t)

    def wave(t):
        for j in range(1, NK):
            if j <= NS:
                if t > 4:
                    continue
                arrivals = [n for n in (2 * t, 2 * t - 1) if 1 <= n <= NZ - 1]
                relay, leave = 2 * t, [n for n in (2 * t + 2, 2 * t + 1) if n <= NZ - 1]
            else:
                arrivals = [t] if t >= 1 else []
                relay, leave = t, [t + 1] if t + 1 <= NZ - 1 else []
            for n in arrivals:
                for side in range(2):
                    line_get(j, side, n)
                    if n == relay:
                        for m in leave:
                            line_send(j, side, m)
                if j <= NB:
                    for side in range(2):
                        line_ring(j, side, n)
            if t == 0:
                for m in leave:
                    for side in range(2):
                        line_send(j, side, m)
                if j <= NB:
                    to_ring(j, zl)

    def direct(t):
        for side in range(2):
            step = 1 if side == 0 else -1

            @pl.when(line_gets(side, t))
            def _():
                p = zl - step * t
                arrived(xs.at[x, 0, rows_of(p)], d_r.at[p])
                to_ring(0, p)

    def ring_in(d):
        q = (x + 4 - d) % 4
        arrived(xs.at[q, 0], b_r.at[d])
        partial(q, 0)

    def permute(q):
        if q == 0:
            loads[2].wait()
        for k in range(NK):
            lo, hi = tile_columns(lambda at, n: w[:, q * QUARTER + at : q * QUARTER + at + n], k)
            wp[q, k, :, 0:128] = lo
            wp[q, k, :, 128:256] = hi

    def partial(q, j):
        value = jnp.dot(ht[...], xs[q, j], preferred_element_type=F32)
        lo, hi = value[:, 0:128], value[:, 128:256]
        pm[q, j] = jnp.where(core == 0, lo, hi)
        csend[q, j] = jnp.where(core == 0, hi, lo).astype(BF)
        send(csend.at[q, j], crecv.at[q, j], c_s.at[q, j], c_r.at[q, j], other)

    left, right, far = (x + 3) % 4, (x + 1) % 4, (x + 2) % 4
    up_half, down_half = pl.ds(0, TOK // 2), pl.ds(TOK // 2, TOK // 2)

    def op_a(j):
        for n, half, d in ((0, up_half, 1), (1, down_half, 3), (4, down_half, 1), (5, up_half, 3)):
            block = xs.at[x, j, half]
            send(block, block, x_s.at[n, j], x_r.at[n, j], at_x(d))
        partial(x, j)

    def op_d(j):
        arrived(xs.at[left, j] if j <= NB else xs.at[left, j, up_half], x_r.at[0, j])
        block = xs.at[left, j, up_half]
        send(block, block, x_s.at[2, j], x_r.at[2, j], at_x(1))
        arrived(xs.at[right, j] if j <= NB else xs.at[right, j, down_half], x_r.at[1, j])
        block = xs.at[right, j, down_half]
        send(block, block, x_s.at[3, j], x_r.at[3, j], at_x(3))
        if j > NB:
            arrived(xs.at[left, j, down_half], x_r.at[4, j])
            arrived(xs.at[right, j, up_half], x_r.at[5, j])
        partial(left, j)
        partial(right, j)

    def op_e(j):
        arrived(xs.at[far, j, up_half], x_r.at[2, j])
        arrived(xs.at[far, j, down_half], x_r.at[3, j])
        partial(far, j)

    lo_r, hi_r = pl.ds(0, HALF), pl.ds(HALF, HALF)

    def op_f(j):
        for q in range(4):
            arrived(crecv.at[q, j], c_r.at[q, j])
        for d in (2, 1, 3):
            q = (y + d) % 4
            ys[d - 1, j] = (pm[q, j] + crecv[q, j].astype(F32)).astype(BF)
            send(ys.at[d - 1, j], yr.at[d - 1, j], y_s.at[d - 1, j], y_r.at[d - 1, j], at_y(d))

    def reduced(j):
        total = pm[y, j] + crecv[y, j].astype(F32)
        for d in (1, 3, 2):
            arrived(yr.at[d - 1, j], y_r.at[d - 1, j])
            total = total + yr[d - 1, j].astype(F32)
        return total

    z_far, z_next, z_prev = (zh + 2) % 4, (zh + 1) % 4, (zh + 3) % 4

    def op_h(j):
        total = reduced(j)
        if j == 0:
            z1s[...] = total.astype(BF)
            send(z1s.at[lo_r], z1r.at[lo_r], z_s.at[0], z_r.at[0], at_z(1))
            send(z1s.at[hi_r], z1r.at[hi_r], z_s.at[1], z_r.at[1], at_z(3))
        elif j == 1:
            zf[0] = total
            z2s[0, hi_r] = total[HALF:].astype(BF)
            send(z2s.at[0, hi_r], z2r.at[0, hi_r], z_s.at[2], z_r.at[2], at_z(1))
        elif j == 2:
            zf[1] = total
            z2s[1, lo_r] = total[:HALF].astype(BF)
            send(z2s.at[1, lo_r], z2r.at[1, lo_r], z_s.at[3], z_r.at[3], at_z(3))
        elif j == 3:
            for o in range(4):
                pr[o] = jnp.concatenate(
                    [total[RR * n : RR * n + RR, 32 * o : 32 * o + 32] for n in range(4)], axis=1
                )
            q1s[...] = pr[z_far].astype(BF)
            send(q1s.at[c0], q1r.at[c0], z_s.at[6], z_r.at[6], at_z(1))
            send(q1s.at[c1], q1r.at[c1], z_s.at[7], z_r.at[7], at_z(3))
            q2s[0, c1] = pr[z_next, c1].astype(BF)
            send(q2s.at[0, c1], q2r.at[0, c1], z_s.at[8], z_r.at[8], at_z(1))
            q2s[1, c0] = pr[z_prev, c0].astype(BF)
            send(q2s.at[1, c0], q2r.at[1, c0], z_s.at[9], z_r.at[9], at_z(3))
        else:
            zf[2] = total

    c0, c1 = pl.ds(0, R0), pl.ds(R0, RR - R0)

    def z_clockwise():
        arrived(z1r.at[lo_r], z_r.at[0])
        z2s[0, lo_r] = (zf[0, lo_r] + z1r[lo_r].astype(F32)).astype(BF)
        send(z2s.at[0, lo_r], z2r.at[0, lo_r], z_s.at[4], z_r.at[4], at_z(1))

    def z_back():
        arrived(z1r.at[hi_r], z_r.at[1])
        z2s[1, hi_r] = (zf[1, hi_r] + z1r[hi_r].astype(F32)).astype(BF)
        send(z2s.at[1, hi_r], z2r.at[1, hi_r], z_s.at[5], z_r.at[5], at_z(3))

    def z_rest():
        arrived(q1r.at[c0], z_r.at[6])
        q2s[0, c0] = (pr[z_next, c0] + q1r[c0].astype(F32)).astype(BF)
        send(q2s.at[0, c0], q2r.at[0, c0], z_s.at[10], z_r.at[10], at_z(1))
        arrived(q1r.at[c1], z_r.at[7])
        q2s[1, c1] = (pr[z_prev, c1] + q1r[c1].astype(F32)).astype(BF)
        send(q2s.at[1, c1], q2r.at[1, c1], z_s.at[11], z_r.at[11], at_z(3))

    def back(j):
        value = None
        for q in range(4):
            term = lax.dot_general(
                wp[q, order[j]], xs[q, j], (((1,), (1,)), ((), ())), preferred_element_type=F32
            )
            value = term if value is None else value + term
        if j == 0:
            bg[...] = value
        else:
            bg[...] += value

    wave(0)
    loads[0].wait()
    loads[1].wait()
    g = gate[...].astype(F32)
    ht[...] = (g * jax.nn.sigmoid(g) * up[...].astype(F32)).astype(BF)
    direct(1)
    direct(2)
    wave(1)
    direct(3)
    direct(4)
    direct(5)
    wave(2)
    direct(6)
    direct(7)
    partial(x, 0)
    wave(3)
    ring_in(1)
    ring_in(3)
    wave(4)
    partial(x, 1)
    ring_in(2)
    op_f(0)
    wave(5)
    op_d(1)
    wave(6)
    partial(x, 2)
    op_d(2)
    wave(7)
    op_a(3)
    op_e(1)
    op_a(4)
    op_h(0)
    op_f(1)
    op_e(2)
    op_f(2)
    op_h(1)
    op_d(3)
    op_h(2)
    op_e(3)
    z_clockwise()
    op_f(3)
    z_back()
    op_d(4)
    op_h(3)
    op_e(4)
    op_f(4)
    permute(0)
    permute(1)
    op_h(4)
    z_rest()
    permute(2)
    permute(3)
    back(0)
    back(1)
    back(2)
    back(3)
    back(4)

    gate_wide = gate[...].astype(F32)
    up_wide = up[...].astype(F32)
    sig = jax.nn.sigmoid(gate_wide)
    back_grad = bg[...]
    ug[...] = (back_grad * (gate_wide * sig)).astype(BF)
    gg[...] = (back_grad * up_wide * sig * (1.0 + gate_wide * (1.0 - sig))).astype(BF)

    factor = jnp.float32(float(TOK * 32) ** -0.5)
    for n in (2, 4):
        arrived(z2r.at[0, hi_r if n == 2 else lo_r], z_r.at[n])
        arrived(z2r.at[1, lo_r if n == 2 else hi_r], z_r.at[n + 1])
    wg[0:128] = ((zf[2] + z2r[0].astype(F32) + z2r[1].astype(F32)) * factor).T
    arrived(q2r.at[0, c1], z_r.at[8])
    arrived(q2r.at[1, c0], z_r.at[9])
    arrived(q2r.at[0, c0], z_r.at[10])
    arrived(q2r.at[1, c1], z_r.at[11])
    rest = ((pr[zh] + q2r[0].astype(F32) + q2r[1].astype(F32)) * factor).T
    wg[128:WIDE] = jnp.concatenate([rest[32 * n : 32 * n + 32] for n in range(4)], axis=1)

    for copy in drains:
        copy.wait_send()
    others = xs.at[0, 0, pl.ds(0, (NZ - 1) * LINE)]
    remote(others, others, d_s.at[0], d_s.at[0], other).wait_send()
    whole = xs.at[x, 0]
    for d in (1, 2, 3):
        remote(whole, whole, b_s.at[d], b_s.at[d], other).wait_send()
    for j in range(1, NB + 1):
        for n in (0, 1):
            remote(whole, whole, x_s.at[n, j], x_s.at[n, j], other).wait_send()
    for j in range(1, NK):
        for side in range(2):
            for t in range(1, NZ):

                @pl.when(line_sends(j, side, t))
                def _():
                    line_copy(j, side, t).wait_send()


def write_out(a, b, c, a_out, b_out, c_out):
    a_out[...] = a[...]
    b_out[...] = b[...]
    c_out[...] = c[...]


def per_device(out_grad, gate_pre, up_pre, down_weight):
    vmem, dma = pltpu.VMEM, pltpu.SemaphoreType.DMA
    anywhere = pl.BlockSpec(memory_space=pl.ANY)
    local = pl.BlockSpec(memory_space=pltpu.VMEM)
    sizes = (
        jax.ShapeDtypeStruct((FFL, TOK), BF),
        jax.ShapeDtypeStruct((FFL, TOK), BF),
        jax.ShapeDtypeStruct((WIDE, FFL), F32),
    )
    parts = pl.pallas_call(
        kernel,
        out_shape=sizes,
        in_specs=[local, anywhere, anywhere, anywhere],
        out_specs=(local, local, local),
        scratch_shapes=[
            vmem((FFL, TOK), BF),
            vmem((FFL, TOK), BF),
            vmem((FFL, 4 * QUARTER), BF),
            vmem((4, NK, FFL, 256), BF),
            vmem((FFL, TOK), BF),
            vmem((4, NK, TOK, 256), BF),
            vmem((4, NK, 16, 256), BF),
            vmem((4, NK, 16, 256), BF),
            vmem((FFL, TOK), F32),
            vmem((4, NK, FFL, 128), F32),
            vmem((4, NK, FFL, 128), BF),
            vmem((4, NK, FFL, 128), BF),
            vmem((3, NK, FFL, 128), BF),
            vmem((3, NK, FFL, 128), BF),
            vmem((FFL, 128), BF),
            vmem((FFL, 128), BF),
            vmem((2, FFL, 128), BF),
            vmem((2, FFL, 128), BF),
            vmem((3, FFL, 128), F32),
            vmem((4, RR, 128), F32),
            vmem((RR, 128), BF),
            vmem((RR, 128), BF),
            vmem((2, RR, 128), BF),
            vmem((2, RR, 128), BF),
            dma((3,)),
            dma((2, 4)),
            dma((2, 4)),
            dma((1,)),
            dma((NZ,)),
            dma((2, NK, NZ)),
            dma((2, NK, NZ)),
            dma((4,)),
            dma((4,)),
            dma((6, NK)),
            dma((6, NK)),
            dma((4, NK)),
            dma((4, NK)),
            dma((3, NK)),
            dma((3, NK)),
            dma((12,)),
            dma((12,)),
        ],
        compiler_params=pltpu.CompilerParams(
            collective_id=0, has_side_effects=True, vmem_limit_bytes=56 * 2**20
        ),
        cost_estimate=pl.CostEstimate(
            flops=4 * TOK * FFL * 4 * QUARTER, bytes_accessed=7 * 2**20, transcendentals=2 * TOK * FFL
        ),
    )(out_grad, gate_pre.T, up_pre.T, down_weight)
    gate_grad, up_grad, weight_grad = pl.pallas_call(
        write_out,
        out_shape=sizes,
        in_specs=[local] * 3,
        out_specs=(local,) * 3,
    )(*parts)
    return gate_grad.T, up_grad.T, weight_grad.T


def solution(mesh):
    placed = (P(("dp", "tensor"), None), P("dp", "tensor"), P("dp", "tensor"), P("tensor", None))
    return jax.shard_map(
        per_device,
        mesh=mesh,
        in_specs=placed,
        out_specs=(P("dp", "tensor"), P("dp", "tensor"), P("tensor", "dp")),
        check_vma=False,
    )
```
